32 devices in a mesh: groups: 1, patch: 16 (over z, y, x), image: 2 (over core).
Axes of the slice: x: 2, y: 2, z: 4, core: 2. Of those that a mesh axis runs over, the one named last changes fastest.
Arguments:
- queries: bfloat16 [2, 128, 1280], P(('groups', 'image'), 'patch'), may hold values from -12 to 12
- fresh_keys: bfloat16 [2, 128, 1280], P(('groups', 'image'), 'patch'), may hold values from -4 to 4
- fresh_values: bfloat16 [2, 128, 1280], P(('groups', 'image'), 'patch'), may hold values from -4 to 4
- stale_keys: bfloat16 [2, 128, 1280], P(('groups', 'image'), 'patch'), may hold values from -12 to 12
- stale_values: bfloat16 [2, 128, 1280], P(('groups', 'image'), 'patch'), may hold values from -4 to 4
- residual: bfloat16 [2, 128, 2560], P(('groups', 'image'), 'patch'), may hold values from -6 to 6
- out_proj: bfloat16 [1280, 2560], P('image'), may hold values from -0.15625 to 0.15625
- norm_gain: float32 [2560], replicated, may hold values from 0.25 to 1.75
- router: float32 [2560, 4], replicated, may hold values from -0.125 to 0.125
- expert_ids: int32 [2, 128, 2], P(('groups', 'image'), 'patch'), may hold values from 0 to 3, all different within a row; in each aligned block of 8 rows (0 to 7, 8 to 15, ..., all dimensions but the last counted through in order) at most 8 rows name the same one
- routed_gate: bfloat16 [16, 384, 2560], P('patch', 'image'), may hold values from -0.125 to 0.125
- routed_up: bfloat16 [16, 384, 2560], P('patch', 'image'), may hold values from -0.125 to 0.125
- routed_down: bfloat16 [16, 384, 2560], P('patch', 'image'), may hold values from -0.15625 to 0.15625
- shared_gate: bfloat16 [768, 2560], P('image'), may hold values from -0.125 to 0.125
- shared_up: bfloat16 [768, 2560], P('image'), may hold values from -0.125 to 0.125
- shared_down: bfloat16 [768, 2560], P('image'), may hold values from -0.21875 to 0.21875
Outputs:
- attended: bfloat16 [2, 128, 2560], P(('groups', 'image'), 'patch')
- block_out: bfloat16 [2, 128, 2560], P(('groups', 'image'), 'patch')
The draws below stay inside these ranges and needn't reach their ends.
Inputs may be any that keep to these rules, and one draw needn't show every extreme that they name: `expert_ids`: each token names two different experts and every expert is named by some token. Among the 8 tokens of one device (aligned blocks of rows, images before positions) no expert is named more than 8 times, a bound that some block reaches.
All inputs are finite; a program needn't handle non-finite values.
Results may differ from the reference program's by a relative error of at most 0.017.
Values may be sent and summed in bfloat16 or wider, within the bound.
A program may use at most 64 MiB of HBM per device.

```python
import math
import jax
import jax.numpy as jnp
import numpy as np
from jax import lax

D = 2560
HD = 128
HID = 1536
SHARED = 768
PATCH_DEV = 8
HH = 1280
SEQ = 128
IMAGES = 2
EXPERTS = 4
CAP = 8
N_PATCH = 16
N_IMAGE = 2


def draw_queries(key, part):
    key = jax.random.fold_in(key, 11)
    return jnp.clip(2.0 * jax.random.normal(key, (IMAGES, SEQ, HH), jnp.float32), -8.0, 8.0).astype(jnp.bfloat16)


def draw_stale_keys(key, part):
    key = jax.random.fold_in(key, 23)
    return jnp.clip(jax.random.normal(key, (IMAGES, SEQ, HH), jnp.float32), -4.0, 4.0).astype(jnp.bfloat16)


def levels(rng, shape, shards, smallest, high):
    def one(position, blocks):
        draws = jax.random.uniform(jax.random.fold_in(jax.random.fold_in(rng, 6), position), (blocks,), jnp.float32, smallest / len(shards), high / len(shards))
        return jnp.repeat(jnp.exp(draws), shape[position] // blocks).reshape((-1,) + (1,) * (len(shape) - position - 1))

    level = one(*shards[0])
    for cut in shards[1:]:
        level = level * one(*cut)
    return level


def deal_out(rng, own, number, rows, number_of, top, limit, skew):
    sequence = jax.random.permutation(rng, number_of)
    packed, ordinary = load_shares(number_of, rows * top, limit, skew, True), load_shares(number_of, rows * top, limit, skew, False)
    places = jnp.arange(number_of)

    def named(sizes, offset_by):
        used = int((sizes > 0).sum())
        fixed = max(1, used // 4)
        passed = fixed + (places - fixed + offset_by * (used - fixed)) % max(1, number_of - fixed)
        return jnp.zeros((number_of,), jnp.int32).at[sequence[jnp.where(places < fixed, places, passed)]].set(jnp.asarray(sizes, jnp.int32))

    sizes = jnp.where(number % 4 == 0, named(packed, number // 4), named(ordinary, number - number // 4 - 1))
    mixed = jax.random.permutation(jax.random.fold_in(own, 3), number_of)
    source_of, taker = mixed[0:number_of // 2 * 2:2], mixed[1:number_of // 2 * 2:2]
    room = jnp.minimum(sizes[source_of] - 1, limit - sizes[taker]) // 2
    room = jnp.where((source_of == sequence[0]) | (taker == sequence[0]) | (sizes[taker] == 0), 0, jnp.maximum(room, 0))
    passed = jax.random.randint(jax.random.fold_in(own, 4), (number_of // 2,), 0, 1 << 20) % (room + 1)
    sizes = sizes.at[source_of].add(-passed).at[taker].add(passed)
    items = jnp.searchsorted(jnp.cumsum(sizes), jnp.arange(rows * top), side="right").astype(jnp.int32)
    table = items.reshape(top, rows).T
    table = table[jax.random.permutation(jax.random.fold_in(own, 1), rows)]
    offset_by = jax.random.randint(jax.random.fold_in(own, 2), (rows, 1), 0, top)
    return jnp.take_along_axis(table, (jnp.arange(top)[None, :] + offset_by) % top, axis=1)


def load_shares(amount, total, most, slope, full):
    loads = [(1 << 20) // math.isqrt(grade ** slope) + 1 for grade in range(1, amount + 1)]
    largest = most if full else min(most, max(-(-total // amount), total * loads[0] // sum(loads)))
    least = 1 if total - largest >= amount - 1 else 0
    given, surplus = [largest] + [least] * (amount - 1), total - largest - least * (amount - 1)
    while surplus > 0:
        free = [i for i in range(1, amount) if given[i] < largest] or [i for i in range(1, amount) if given[i] < most]
        whole, left = sum([loads[i] for i in free]), surplus
        for i in free:
            addition = min(most - given[i], max(1, left * loads[i] // whole), surplus)
            given[i] = given[i] + addition
            surplus = surplus - addition
    return np.array(given)


def centred(rng, shape, scale, reach, cuts=(), held_as=jnp.bfloat16):
    drawn = scale * jax.random.normal(rng, shape, jnp.float32)
    if cuts:
        drawn = drawn * levels(rng, shape, cuts, -0.22, 0.18)
    return jnp.clip(drawn, -reach, reach).astype(held_as)


def setup_inputs(seed: int = 0, part: int = 0) -> dict:
    splits = jax.random.split(jax.random.key(seed), 17)
    part_splits = jax.random.split(jax.random.fold_in(splits[16], part), 17)
    queries = draw_queries(jax.random.fold_in(jax.random.fold_in(splits[16], part), 71), part)
    fresh_keys = centred(part_splits[1], (IMAGES, SEQ, HH), 1.0, 4.0, ((0, 2), (1, 16)))
    fresh_values = centred(part_splits[2], (IMAGES, SEQ, HH), 1.0, 4.0, ((0, 2), (1, 16)))
    stale_keys = draw_stale_keys(jax.random.fold_in(jax.random.fold_in(splits[16], part), 71), part)
    stale_values = centred(part_splits[4], (IMAGES, SEQ, HH), 1.0, 4.0, ((0, 2), (1, 16)))
    residual = centred(part_splits[5], (IMAGES, SEQ, D), 1.0, 6.0, ((0, 2), (1, 16)))
    out_proj = centred(splits[6], (HH, D), HH ** -0.5, 0.15625, ((0, 2),))
    norm_gain = jnp.clip(1.0 + 0.15 * jax.random.normal(splits[7], (D,), jnp.float32), 0.25, 1.75)
    router = centred(splits[8], (D, EXPERTS), D ** -0.5, 0.125, (), jnp.float32)
    expert_ids_keys = jax.random.split(jax.random.fold_in(part_splits[9], 1), IMAGES * SEQ // PATCH_DEV)
    expert_ids_turns = jax.random.permutation(jax.random.fold_in(part_splits[9], 3), IMAGES * SEQ // PATCH_DEV)
    expert_ids = jax.vmap(lambda own, number: deal_out(jax.random.fold_in(part_splits[9], 2), own, number, PATCH_DEV, EXPERTS, 2, CAP, 2))(expert_ids_keys, expert_ids_turns).reshape((IMAGES, SEQ, 2))
    routed_gate = centred(splits[10], (EXPERTS * 4, HID // 4, D), D ** -0.5, 0.125, ((0, 16), (1, 2)))
    routed_up = centred(splits[11], (EXPERTS * 4, HID // 4, D), D ** -0.5, 0.125, ((0, 16), (1, 2)))
    routed_down = centred(splits[12], (EXPERTS * 4, HID // 4, D), HID ** -0.5, 0.15625, ((0, 16), (1, 2)))
    shared_gate = centred(splits[13], (SHARED, D), D ** -0.5, 0.125, ((0, 2),))
    shared_up = centred(splits[14], (SHARED, D), D ** -0.5, 0.125, ((0, 2),))
    shared_down = centred(splits[15], (SHARED, D), SHARED ** -0.5, 0.21875, ((0, 2),))
    return dict(queries=queries, fresh_keys=fresh_keys, fresh_values=fresh_values, stale_keys=stale_keys, stale_values=stale_values, residual=residual, out_proj=out_proj, norm_gain=norm_gain, router=router, expert_ids=expert_ids, routed_gate=routed_gate, routed_up=routed_up, routed_down=routed_down, shared_gate=shared_gate, shared_up=shared_up, shared_down=shared_down)


EPS = 1e-06

def attend_patch(query_rows, key_rows, value_rows):
    factor = HD ** (-0.5)
    scores = jnp.einsum('qhd,khd->hqk', query_rows.astype(jnp.float32), key_rows.astype(jnp.float32)) * factor
    row_max = lax.optimization_barrier(jnp.max(scores, axis=-1, keepdims=True))
    exp_scores = jnp.exp(scores - row_max)
    exp_total = lax.optimization_barrier(jnp.sum(exp_scores, axis=-1))
    weights = lax.optimization_barrier(exp_scores.astype(jnp.bfloat16)).astype(jnp.float32)
    weighted = jnp.einsum('hqk,khd->qhd', weights, value_rows.astype(jnp.float32))
    return (weighted / jnp.transpose(exp_total)[:, :, None]).astype(jnp.bfloat16)

def attention(queries, fresh_keys, fresh_values, stale_keys, stale_values):
    head_count = queries.shape[-1] // HD

    def one_block(block_number):
        image_index = block_number // N_PATCH
        row_start = block_number % N_PATCH * PATCH_DEV

        def pick_image(stacked):
            return lax.dynamic_index_in_dim(stacked, image_index, 0, keepdims=False).reshape(SEQ, head_count, HD)
        query_rows = lax.dynamic_slice_in_dim(pick_image(queries), row_start, PATCH_DEV, 0)
        key_rows = lax.dynamic_update_slice_in_dim(pick_image(stale_keys), lax.dynamic_slice_in_dim(pick_image(fresh_keys), row_start, PATCH_DEV, 0), row_start, 0)
        value_rows = lax.dynamic_update_slice_in_dim(pick_image(stale_values), lax.dynamic_slice_in_dim(pick_image(fresh_values), row_start, PATCH_DEV, 0), row_start, 0)
        return attend_patch(query_rows, key_rows, value_rows)
    blocks = jnp.arange(IMAGES * N_PATCH, dtype=jnp.int32)
    return lax.map(one_block, blocks).reshape(IMAGES, SEQ, head_count * HD)

def project_rows(in_rows, weight_rows):
    return lax.dot_general(in_rows, weight_rows, (((1,), (1,)), ((), ())), preferred_element_type=jnp.float32)

def swiglu_rows(in_rows, gate_rows, up_rows):
    gate_vals = project_rows(in_rows, gate_rows)
    up_vals = project_rows(in_rows, up_rows)
    return (jax.nn.silu(gate_vals) * up_vals).astype(jnp.bfloat16)

def expert_block(expert_rows, gate_rows, up_rows, down_rows):
    hidden = swiglu_rows(expert_rows, gate_rows, up_rows)
    shard_count = 4 * N_IMAGE
    row_count = hidden.shape[0]
    pieces = jnp.einsum('rsk,skd->rsd', hidden.reshape(row_count, shard_count, -1).astype(jnp.float32), down_rows.reshape(shard_count, -1, down_rows.shape[-1]).astype(jnp.float32))
    rounded = lax.optimization_barrier(pieces.astype(jnp.bfloat16)).astype(jnp.float32)
    return lax.optimization_barrier(jnp.sum(rounded, axis=1))

def count_slots(block_ids):
    onehot = (block_ids[:, None] == jnp.arange(EXPERTS, dtype=jnp.int32)[None, :]).astype(jnp.int32)
    earlier = jnp.cumsum(onehot, axis=0) - onehot
    return lax.optimization_barrier(jnp.sum(earlier * onehot, axis=1)).astype(jnp.int32)

def reference(queries, fresh_keys, fresh_values, stale_keys, stale_values, residual, out_proj, norm_gain, router, expert_ids, routed_gate, routed_up, routed_down, shared_gate, shared_up, shared_down):
    heads_out = attention(queries, fresh_keys, fresh_values, stale_keys, stale_values)
    model_width = residual.shape[-1]
    projected = jnp.dot(heads_out.reshape(-1, heads_out.shape[-1]), out_proj, preferred_element_type=jnp.float32)
    attended = (residual.reshape(-1, model_width).astype(jnp.float32) + projected).astype(jnp.bfloat16)
    mid_f32 = attended.astype(jnp.float32)
    mean_sq = lax.optimization_barrier(jnp.mean(mid_f32 * mid_f32, axis=-1, keepdims=True))
    normed = (mid_f32 * lax.rsqrt(mean_sq + EPS) * norm_gain).astype(jnp.bfloat16)
    logits = jnp.dot(normed.astype(jnp.float32), router, precision=lax.Precision.HIGHEST)
    gate_probs = jax.nn.sigmoid(logits)
    blocks = IMAGES * N_PATCH
    chosen_ids = expert_ids.reshape(-1, 2)
    pair_weight = jnp.take_along_axis(gate_probs, chosen_ids, axis=1).reshape(blocks, 2 * PATCH_DEV)
    block_ids = expert_ids.reshape(blocks, 2 * PATCH_DEV)
    slot_of = jax.vmap(count_slots)(block_ids)
    block_index = jnp.broadcast_to(jnp.arange(blocks, dtype=jnp.int32)[:, None], block_ids.shape)
    pair_rows = jnp.repeat(normed.reshape(blocks, PATCH_DEV, model_width), 2, axis=1)
    buffer = jnp.zeros((EXPERTS, blocks, CAP, model_width), jnp.bfloat16).at[block_ids, block_index, slot_of].set(pair_rows)
    hid_total = 4 * routed_gate.shape[1]
    gate_full = routed_gate.reshape(EXPERTS, hid_total, model_width)
    up_full = routed_up.reshape(EXPERTS, hid_total, model_width)
    down_full = routed_down.reshape(EXPERTS, hid_total, model_width)

    def run_expert(operands):
        expert_rows, gate_rows, up_rows, down_rows = operands
        return expert_block(expert_rows.reshape(-1, model_width), gate_rows, up_rows, down_rows)
    expert_out = lax.map(run_expert, (buffer, gate_full, up_full, down_full)).reshape(EXPERTS, blocks, CAP, model_width)
    pair_out = expert_out[block_ids, block_index, slot_of]
    routed = lax.optimization_barrier(jnp.sum((pair_weight[..., None] * pair_out).reshape(blocks * PATCH_DEV, 2, model_width), axis=1))
    shared_hidden = swiglu_rows(normed, shared_gate, shared_up)
    shared_out = jnp.dot(shared_hidden, shared_down, preferred_element_type=jnp.float32)
    block_out = (mid_f32 + shared_out + routed).astype(jnp.bfloat16)
    return (attended.reshape(IMAGES, SEQ, model_width), block_out.reshape(IMAGES, SEQ, model_width))
```

```python
import functools

import jax
import jax.numpy as jnp
from jax import lax
from jax.experimental import pallas as pl
from jax.experimental.pallas import tpu as pltpu
from jax.sharding import PartitionSpec as P

HD = 128
EPS = 1e-06
MEMBERS = 4
MESH = pl.DeviceIdType.MESH
F32 = jnp.float32
BF16 = jnp.bfloat16


def dot_nt(rows, weight):
    return lax.dot_general(rows, weight, (((1,), (1,)), ((), ())), preferred_element_type=F32)


def dot_nn(rows, weight):
    return lax.dot_general(rows, weight, (((1,), (0,)), ((), ())), preferred_element_type=F32)


def stack_halves(rows):
    width = rows.shape[1] // 2
    return jnp.concatenate([rows[:, :width], rows[:, width:]], axis=0).astype(BF16)


def unstack_halves(packed):
    rows = packed.astype(F32)
    count = rows.shape[0] // 2
    return jnp.concatenate([rows[:count], rows[count:]], axis=1)


def send_count(groups):
    others = groups - 1
    members = MEMBERS - 1
    kv = 4 + 2 * others + 2 * groups * members
    tokens = 1 + others + groups * members + groups * MEMBERS - 1
    results = 1 + groups + groups * members + 2 * others + 1
    return kv + tokens + results


def kernel(
    groups,
    q_ref, fk_ref, fv_ref, sk_ref, sv_ref, res_ref, gain_ref, router_ref, ids_ref,
    wo_hbm, rg_hbm, ru_hbm, rd_hbm, sg_hbm, su_hbm, sd_hbm,
    att_ref, out_ref,
    wo, rg, ru, rd, sg, su, sd,
    stale_own, sib_kv, sib_q, sib_res, q_x, res_x, kv,
    part_s, part_r, tok, sh_s, sh_r,
    half_s, half_r, half_own, plane_s, plane_r, line_s, line_r,
    w_sem, send_sem, sib_sem, kv_sem, tok_sem, toks_sem, half_sem, plane_sem, line_sem,
):
    patch = lax.axis_index("patch")
    core = lax.axis_index("image")
    other = 1 - core
    first = core == 0
    group = patch // MEMBERS
    member = patch % MEMBERS
    rows = q_ref.shape[1]
    heads_half = q_ref.shape[2] // 2
    width = res_ref.shape[2]
    half = width // 2

    def at(step_group, step_member, to_core):
        target = ((group + step_group) % groups) * MEMBERS + (member + step_member) % MEMBERS
        return {"patch": target, "image": to_core}

    sibling = at(0, 0, other)

    barrier = pltpu.get_barrier_semaphore()
    greeted = [sibling]
    for d in range(1, groups):
        greeted += [at(d, 0, core), at(d, 0, other)]
    for k in range(1, MEMBERS):
        greeted.append(at(0, k, core))
    for target in greeted:
        pl.semaphore_signal(barrier, inc=1, device_id=target, device_id_type=MESH)

    weights = []
    pairs = [(wo_hbm, wo), (sg_hbm, sg), (su_hbm, su), (sd_hbm, sd)]
    pairs += [(rg_hbm, rg), (ru_hbm, ru), (rd_hbm, rd)]
    for number, (src, dst) in enumerate(pairs):
        copy = pltpu.make_async_copy(src, dst, w_sem.at[number])
        copy.start()
        weights.append(copy)

    sent = []

    def send(src, dst, recv, target):
        copy = pltpu.make_async_remote_copy(
            src_ref=src, dst_ref=dst, send_sem=send_sem.at[len(sent)], recv_sem=recv,
            device_id=target, device_id_type=MESH,
        )
        copy.start()
        sent.append(copy)

    def arrived(ref, recv):
        pltpu.make_async_remote_copy(
            src_ref=ref, dst_ref=ref, send_sem=send_sem.at[0], recv_sem=recv,
            device_id=sibling, device_id_type=MESH,
        ).wait_recv()

    def split(ref):
        whole = ref[0].astype(F32)
        left, right = whole[:, :heads_half], whole[:, heads_half:]
        return jnp.where(first, left, right), jnp.where(first, right, left)

    sk_mine, sk_theirs = split(sk_ref)
    sv_mine, sv_theirs = split(sv_ref)
    stale_own[0] = jnp.concatenate([sk_mine, sv_mine], axis=0).astype(BF16)
    sib_kv[0] = jnp.concatenate([sk_theirs, sv_theirs], axis=0).astype(BF16)
    fk_mine, fk_theirs = split(fk_ref)
    fv_mine, fv_theirs = split(fv_ref)
    kv[0, 0, 0] = jnp.concatenate([fk_mine, fv_mine], axis=0).astype(BF16)
    sib_kv[1] = jnp.concatenate([fk_theirs, fv_theirs], axis=0).astype(BF16)
    q_mine, q_theirs = split(q_ref)
    sib_q[...] = q_theirs
    residual = res_ref[0].astype(F32)
    sib_res[...] = residual

    pl.semaphore_wait(barrier, len(greeted))

    send(sib_kv.at[0], stale_own.at[1], sib_sem.at[0], sibling)
    for d in range(1, groups):
        send(stale_own.at[0], kv.at[groups - d, 0, 0], kv_sem.at[groups - d, 0, 0], at(d, 0, core))
        send(sib_kv.at[0], kv.at[groups - d, 0, 1], kv_sem.at[groups - d, 0, 1], at(d, 0, other))
    for k in range(1, MEMBERS):
        send(stale_own.at[0], kv.at[0, MEMBERS - k, 0], kv_sem.at[0, MEMBERS - k, 0], at(0, k, core))
    send(sib_kv.at[1], kv.at[0, 0, 1], kv_sem.at[0, 0, 1], sibling)
    send(sib_q, q_x, sib_sem.at[1], sibling)
    send(sib_res, res_x, sib_sem.at[2], sibling)
    arrived(stale_own.at[1], sib_sem.at[0])
    for k in range(1, MEMBERS):
        send(stale_own.at[1], kv.at[0, MEMBERS - k, 1], kv_sem.at[0, MEMBERS - k, 1], at(0, k, core))
    for d in range(1, groups):
        for i in range(2):
            arrived(kv.at[d, 0, i], kv_sem.at[d, 0, i])
            for k in range(1, MEMBERS):
                send(kv.at[d, 0, i], kv.at[d, MEMBERS - k, i], kv_sem.at[d, MEMBERS - k, i],
                     at(0, k, core))
    arrived(q_x, sib_sem.at[1])
    arrived(res_x, sib_sem.at[2])
    arrived(kv.at[0, 0, 1], kv_sem.at[0, 0, 1])
    for d in range(groups):
        for k in range(1, MEMBERS):
            for i in range(2):
                arrived(kv.at[d, k, i], kv_sem.at[d, k, i])

    heads = heads_half // HD
    key_rows = groups * MEMBERS * 2 * rows
    row_head = lax.broadcasted_iota(jnp.int32, (heads * rows, heads_half), 0) // rows
    lane_head = lax.broadcasted_iota(jnp.int32, (heads * rows, heads_half), 1) // HD
    own_head = row_head == lane_head
    is_key = lax.broadcasted_iota(jnp.int32, (heads * rows, key_rows), 1) % (2 * rows) < rows
    outs = []
    for i, query in enumerate((q_mine, q_x[...])):
        block = kv[:, :, i].reshape(key_rows, heads_half)
        spread = jnp.where(own_head, jnp.concatenate([query] * heads, axis=0), 0.0).astype(BF16)
        scores = dot_nt(spread, block) * (HD ** -0.5)
        scores = jnp.where(is_key, scores, -1e30)
        top = jnp.max(scores, axis=-1, keepdims=True)
        exp_scores = jnp.where(is_key, jnp.exp(scores - top), 0.0)
        total = jnp.sum(exp_scores, axis=-1, keepdims=True)
        moved = pltpu.roll(exp_scores, rows, axis=1).astype(BF16)
        mixed = dot_nn(moved, block) / total
        outs.append(jnp.concatenate(
            [mixed[h * rows:(h + 1) * rows, h * HD:(h + 1) * HD] for h in range(heads)], axis=1))

    def by_image(mine, theirs):
        return jnp.concatenate(
            [jnp.where(first, mine, theirs), jnp.where(first, theirs, mine)], axis=0)

    def own_rows(both):
        return jnp.where(first, both[:rows], both[rows:])

    def other_rows(both):
        return jnp.where(first, both[rows:], both[:rows])

    weights[0].wait()
    part_s[...] = dot_nn(by_image(outs[0], outs[1]).astype(BF16), wo[...])
    send(part_s, part_r, sib_sem.at[3], sibling)
    arrived(part_r, sib_sem.at[3])
    projected = part_s[...] + part_r[...]
    attended = (by_image(residual, res_x[...]) + projected).astype(BF16).astype(F32)
    mean_sq = jnp.mean(attended * attended, axis=-1, keepdims=True)
    normed32 = attended * lax.rsqrt(mean_sq + EPS) * gain_ref[...]
    normed = normed32.astype(BF16)
    tok[0, 0, 0] = normed[:, :half]
    tok[0, 0, 1] = normed[:, half:]

    own = tok.at[0, 0, core]
    for d in range(1, groups):
        send(own, tok.at[groups - d, 0, core], tok_sem.at[groups - d, 0], at(d, 0, core))
    for k in range(1, MEMBERS):
        send(own, tok.at[0, MEMBERS - k, core], tok_sem.at[0, MEMBERS - k], at(0, k, core))

    mid = own_rows(attended)
    att_ref[0] = mid.astype(BF16)
    for number in (1, 2, 3):
        weights[number].wait()
    hidden = jax.nn.silu(dot_nt(normed, sg[...])) * dot_nt(normed, su[...])
    shared = dot_nn(hidden.astype(BF16), sd[...])
    sh_s[...] = stack_halves(other_rows(shared))
    send(sh_s, sh_r, sib_sem.at[4], sibling)

    for d in range(1, groups):
        arrived(tok.at[d, 0, core], tok_sem.at[d, 0])
        for k in range(1, MEMBERS):
            send(tok.at[d, 0, core], tok.at[d, MEMBERS - k, core], tok_sem.at[d, MEMBERS - k],
                 at(0, k, core))
        send(tok.at[d, 0, core], tok.at[d, 0, core], toks_sem.at[d, 0], sibling)

    mine_normed = own_rows(normed.astype(F32))
    logits = lax.dot_general(mine_normed, router_ref[...], (((1,), (1,)), ((), ())),
                             precision=lax.Precision.HIGHEST, preferred_element_type=F32)
    probs = jax.nn.sigmoid(logits)
    experts = lax.broadcasted_iota(jnp.int32, (rows, groups), 1)
    ids = ids_ref[0]
    named = (ids[:, 0:1] == experts) | (ids[:, 1:2] == experts)
    pair_weight = jnp.where(named, probs, 0.0)
    base = mid + own_rows(shared)

    for number in (4, 5, 6):
        weights[number].wait()

    def expert(d):
        for k in range(1, MEMBERS):
            arrived(tok.at[d, k, core], tok_sem.at[d, k])
            send(tok.at[d, k, core], tok.at[d, k, core], toks_sem.at[d, k], sibling)
        for k in range(MEMBERS):
            if d or k:
                arrived(tok.at[d, k, other], toks_sem.at[d, k])
        count = MEMBERS * 2 * rows
        left = tok[d, :, 0].reshape(count, half)
        right = tok[d, :, 1].reshape(count, half)
        gate = dot_nt(left, rg[:, :half]) + dot_nt(right, rg[:, half:])
        up = dot_nt(left, ru[:, :half]) + dot_nt(right, ru[:, half:])
        inner = (jax.nn.silu(gate) * up).astype(BF16)
        out_left = dot_nn(inner, rd[:, :half])
        out_right = dot_nn(inner, rd[:, half:])
        half_own[d] = jnp.where(first, out_left, out_right)
        half_s[d] = jnp.where(first, out_right, out_left).astype(BF16)
        send(half_s.at[d], half_r.at[d], half_sem.at[d], sibling)

    def to_plane(d):
        arrived(half_r.at[d], half_sem.at[d])
        half_own[d] += half_r[d].astype(F32)
        for k in range(1, MEMBERS):
            plane_s[d, k] = half_own[d, pl.ds(k * 2 * rows, 2 * rows)].astype(BF16)
            send(plane_s.at[d, k], plane_r.at[d, MEMBERS - k], plane_sem.at[d, MEMBERS - k],
                 at(0, k, core))

    def to_line(d):
        total = half_own[d, pl.ds(0, 2 * rows)]
        for k in range(1, MEMBERS):
            arrived(plane_r.at[d, k], plane_sem.at[d, k])
            total += plane_r[d, k].astype(F32)
        line_s[d, 1] = stack_halves(other_rows(total))
        back = (groups - d) % groups
        if d == 0:
            line_r[0, core] = stack_halves(own_rows(total))
        else:
            line_s[d, 0] = stack_halves(own_rows(total))
            send(line_s.at[d, 0], line_r.at[back, core], line_sem.at[back, core], at(d, 0, core))
        send(line_s.at[d, 1], line_r.at[back, core], line_sem.at[back, core], at(d, 0, other))

    order = list(range(groups))
    for step in range(groups + 2):
        if step < groups:
            expert(order[step])
        if 0 <= step - 1 < groups:
            to_plane(order[step - 1])
        if 0 <= step - 2 < groups:
            to_line(order[step - 2])

    arrived(sh_r, sib_sem.at[4])
    result = base + unstack_halves(sh_r[...])
    for d in order:
        if d == 0:
            arrived(line_r.at[0, other], line_sem.at[0, other])
        else:
            arrived(line_r.at[d, 0], line_sem.at[d, 0])
            arrived(line_r.at[d, 1], line_sem.at[d, 1])
        column = jnp.where(experts == (group + d) % groups, pair_weight, 0.0)
        scale = jnp.sum(column, axis=1, keepdims=True)
        value = jnp.concatenate(
            [unstack_halves(line_r[d, 0]), unstack_halves(line_r[d, 1])], axis=1)
        result += scale * value
    out_ref[0] = result.astype(BF16)

    for copy in sent:
        copy.wait_send()


def per_device(
    queries, fresh_keys, fresh_values, stale_keys, stale_values, residual, out_proj, norm_gain,
    router, expert_ids, routed_gate, routed_up, routed_down, shared_gate, shared_up, shared_down,
):
    groups = router.shape[1]
    rows, width = residual.shape[1:]
    half = width // 2
    heads_half = queries.shape[2] // 2
    pack = 2 * rows
    weights = (out_proj, routed_gate[0], routed_up[0], routed_down[0],
               shared_gate, shared_up, shared_down)
    order = (0, 1, 2, 3, 4, 5, 6)
    vmem = pl.BlockSpec(memory_space=pltpu.VMEM)
    hbm = pl.BlockSpec(memory_space=pl.ANY)
    dma = pltpu.SemaphoreType.DMA
    scratch = [pltpu.VMEM(weights[n].shape, BF16) for n in order]
    scratch += [
        pltpu.VMEM((2, pack, heads_half), BF16),
        pltpu.VMEM((2, pack, heads_half), BF16),
        pltpu.VMEM((rows, heads_half), F32),
        pltpu.VMEM((rows, width), F32),
        pltpu.VMEM((rows, heads_half), F32),
        pltpu.VMEM((rows, width), F32),
        pltpu.VMEM((groups, MEMBERS, 2, pack, heads_half), BF16),
        pltpu.VMEM((pack, width), F32),
        pltpu.VMEM((pack, width), F32),
        pltpu.VMEM((groups, MEMBERS, 2, pack, half), BF16),
        pltpu.VMEM((pack, half), BF16),
        pltpu.VMEM((pack, half), BF16),
        pltpu.VMEM((groups, MEMBERS * pack, half), BF16),
        pltpu.VMEM((groups, MEMBERS * pack, half), BF16),
        pltpu.VMEM((groups, MEMBERS * pack, half), F32),
        pltpu.VMEM((groups, MEMBERS, pack, half), BF16),
        pltpu.VMEM((groups, MEMBERS, pack, half), BF16),
        pltpu.VMEM((groups, 2, pack, half // 2), BF16),
        pltpu.VMEM((groups, 2, pack, half // 2), BF16),
        dma((7,)),
        dma((send_count(groups),)),
        dma((5,)),
        dma((groups, MEMBERS, 2)),
        dma((groups, MEMBERS)),
        dma((groups, MEMBERS)),
        dma((groups,)),
        dma((groups, MEMBERS)),
        dma((groups, 2)),
    ]
    return pl.pallas_call(
        functools.partial(kernel, groups),
        out_shape=(
            jax.ShapeDtypeStruct(residual.shape, BF16),
            jax.ShapeDtypeStruct(residual.shape, BF16),
        ),
        in_specs=[vmem] * 9 + [hbm] * 7,
        out_specs=(vmem, vmem),
        scratch_shapes=scratch,
        compiler_params=pltpu.CompilerParams(
            collective_id=0, has_side_effects=True, vmem_limit_bytes=56 * 1024 * 1024
        ),
        name="block",
    )(
        queries, fresh_keys, fresh_values, stale_keys, stale_values, residual,
        norm_gain.reshape(1, width), router.T, expert_ids, *weights,
    )


def solution(mesh):
    tokens = P(("groups", "image"), "patch", None)
    in_specs = (
        (tokens,) * 6
        + (P("image", None), P(), P(), tokens)
        + (P("patch", "image", None),) * 3
        + (P("image", None),) * 3
    )
    return jax.shard_map(
        per_device, mesh=mesh, in_specs=in_specs, out_specs=(tokens, tokens), check_vma=False
    )
```

```python
import functools

import jax
import jax.numpy as jnp
from jax import lax
from jax.experimental import pallas as pl
from jax.experimental.pallas import tpu as pltpu
from jax.sharding import PartitionSpec as P

HD = 128
EPS = 1e-06
MEMBERS = 4
MESH = pl.DeviceIdType.MESH
F32 = jnp.float32
BF16 = jnp.bfloat16


def dot_nt(rows, weight):
    return lax.dot_general(rows, weight, (((1,), (1,)), ((), ())), preferred_element_type=F32)


def dot_nn(rows, weight):
    return lax.dot_general(rows, weight, (((1,), (0,)), ((), ())), preferred_element_type=F32)


def stack_halves(rows):
    width = rows.shape[1] // 2
    return jnp.concatenate([rows[:, :width], rows[:, width:]], axis=0).astype(BF16)


def unstack_halves(packed):
    rows = packed.astype(F32)
    count = rows.shape[0] // 2
    return jnp.concatenate([rows[:count], rows[count:]], axis=1)


def send_count(groups):
    others = groups - 1
    members = MEMBERS - 1
    kv = 4 + 2 * others + 2 * groups * members + others * members
    tokens = 1 + others + groups * members + others * members + groups * MEMBERS - 1
    results = 1 + groups + groups * members + 2 * others + 1
    return kv + tokens + results


def kernel(
    groups,
    q_hbm, fk_hbm, fv_hbm, sk_hbm, sv_hbm, res_hbm, gain_hbm, router_hbm, ids_hbm,
    wo_hbm, rg_hbm, ru_hbm, rd_hbm, sg_hbm, su_hbm, sd_hbm,
    att_ref, out_ref,
    q_ref, fk_ref, fv_ref, sk_ref, sv_ref, res_ref, gain_ref, router_ref, ids_ref,
    wo, rg, ru, rd, sg, su, sd,
    stale_own, sib_kv, sib_q, sib_res, q_x, res_x, kv,
    part_s, part_r, tok, sh_s, sh_r,
    half_s, half_r, half_own, plane_s, plane_r, line_s, line_r,
    in_sem, w_sem, send_sem, sib_sem, kv_sem, rest_sem, tok_sem, tokr_sem, toks_sem, half_sem, plane_sem, line_sem,
):
    patch = lax.axis_index("patch")
    core = lax.axis_index("image")
    other = 1 - core
    first = core == 0
    group = patch // MEMBERS
    member = patch % MEMBERS
    rows = q_ref.shape[1]
    heads_half = q_ref.shape[2] // 2
    width = res_ref.shape[2]
    half = width // 2

    def at(step_group, step_member, to_core):
        target = ((group + step_group) % groups) * MEMBERS + (member + step_member) % MEMBERS
        return {"patch": target, "image": to_core}

    sibling = at(0, 0, other)

    near = jnp.minimum(group, groups - 1 - group)
    forward = 1 - 2 * ((2 * group) // groups)
    steps = [0]
    for s in range(groups - 1):
        both = forward * (1 - 2 * (s % 2)) * (s // 2 + 1)
        rest = forward * (s - near + 1)
        steps.append((jnp.where(s < 2 * near, both, rest) + groups) % groups)

    barrier = pltpu.get_barrier_semaphore()
    greeted = [sibling]
    for d in range(1, groups):
        greeted += [at(d, 0, core), at(d, 0, other)]
    for k in range(1, MEMBERS):
        greeted += [at(0, k, core), at(0, k, other)]
    for target in greeted:
        pl.semaphore_signal(barrier, inc=1, device_id=target, device_id_type=MESH)

    loads = []
    pairs = [(sk_hbm, sk_ref), (sv_hbm, sv_ref), (fk_hbm, fk_ref), (fv_hbm, fv_ref)]
    pairs += [(q_hbm, q_ref), (res_hbm, res_ref), (gain_hbm, gain_ref)]
    pairs += [(router_hbm, router_ref), (ids_hbm, ids_ref)]
    for number, (src, dst) in enumerate(pairs):
        copy = pltpu.make_async_copy(src, dst, in_sem.at[number])
        copy.start()
        loads.append(copy)

    weights = []
    pairs = [(wo_hbm, wo), (sg_hbm, sg), (su_hbm, su), (sd_hbm, sd)]
    pairs += [(rg_hbm, rg), (ru_hbm, ru), (rd_hbm, rd)]
    for number, (src, dst) in enumerate(pairs):
        copy = pltpu.make_async_copy(src, dst, w_sem.at[number])
        copy.start()
        weights.append(copy)

    sent = []

    def send(src, dst, recv, target):
        copy = pltpu.make_async_remote_copy(
            src_ref=src, dst_ref=dst, send_sem=send_sem.at[len(sent)], recv_sem=recv,
            device_id=target, device_id_type=MESH,
        )
        copy.start()
        sent.append(copy)

    def arrived(ref, recv):
        pltpu.make_async_remote_copy(
            src_ref=ref, dst_ref=ref, send_sem=send_sem.at[0], recv_sem=recv,
            device_id=sibling, device_id_type=MESH,
        ).wait_recv()

    def split(ref):
        whole = ref[0].astype(F32)
        left, right = whole[:, :heads_half], whole[:, heads_half:]
        return jnp.where(first, left, right), jnp.where(first, right, left)

    loads[0].wait()
    loads[1].wait()
    sk_mine, sk_theirs = split(sk_ref)
    sv_mine, sv_theirs = split(sv_ref)
    stale_own[...] = jnp.concatenate([sk_mine, sv_mine], axis=0).astype(BF16)
    sib_kv[0] = jnp.concatenate([sk_theirs, sv_theirs], axis=0).astype(BF16)
    for load in loads[2:]:
        load.wait()
    fk_mine, fk_theirs = split(fk_ref)
    fv_mine, fv_theirs = split(fv_ref)
    kv[0, 0, 0] = jnp.concatenate([fk_mine, fv_mine], axis=0).astype(BF16)
    sib_kv[1] = jnp.concatenate([fk_theirs, fv_theirs], axis=0).astype(BF16)
    q_mine, q_theirs = split(q_ref)
    sib_q[...] = q_theirs
    residual = res_ref[0].astype(F32)
    sib_res[...] = residual

    pl.semaphore_wait(barrier, len(greeted))

    cut = heads_half - heads_half // 5
    for d in steps[1:]:
        send(stale_own, kv.at[groups - d, 0, 0], kv_sem.at[groups - d, 0, 0], at(d, 0, core))
        send(sib_kv.at[0], kv.at[groups - d, 0, 1], kv_sem.at[groups - d, 0, 1], at(d, 0, other))
    for k in range(1, MEMBERS):
        back = MEMBERS - k
        send(stale_own, kv.at[0, back, 0], kv_sem.at[0, back, 0], at(0, k, core))
        send(sib_kv.at[0], kv.at[0, back, 1], kv_sem.at[0, back, 1], at(0, k, other))
    send(sib_kv.at[1], kv.at[0, 0, 1], kv_sem.at[0, 0, 1], sibling)
    send(sib_q, q_x, sib_sem.at[1], sibling)
    send(sib_res, res_x, sib_sem.at[2], sibling)

    def kv_part(d, k, i):
        return kv.at[d, k, i, :, pl.ds(0, cut)]

    def kv_rest(d, k):
        return kv.at[d, k, :, :, pl.ds(cut, heads_half - cut)]

    def kv_on(d):
        for i in range(2):
            arrived(kv.at[d, 0, i], kv_sem.at[d, 0, i])
            for k in range(1, MEMBERS):
                back = MEMBERS - k
                send(kv_part(d, 0, i), kv_part(d, back, i), kv_sem.at[d, back, i], at(0, k, core))

    for d in steps[1:2]:
        kv_on(d)
    for k in range(1, MEMBERS):
        for i in range(2):
            arrived(kv.at[0, k, i], kv_sem.at[0, k, i])
        for d in steps[1:]:
            send(kv_rest(0, k), kv_rest(groups - d, k), rest_sem.at[groups - d, k], at(d, 0, core))
    for d in steps[2:]:
        kv_on(d)
    arrived(q_x, sib_sem.at[1])
    arrived(res_x, sib_sem.at[2])
    arrived(kv.at[0, 0, 1], kv_sem.at[0, 0, 1])
    for d in steps[1:]:
        for k in range(1, MEMBERS):
            for i in range(2):
                arrived(kv_part(d, k, i), kv_sem.at[d, k, i])
            arrived(kv_rest(d, k), rest_sem.at[d, k])

    heads = heads_half // HD
    key_rows = groups * MEMBERS * 2 * rows
    row_head = lax.broadcasted_iota(jnp.int32, (heads * rows, heads_half), 0) // rows
    lane_head = lax.broadcasted_iota(jnp.int32, (heads * rows, heads_half), 1) // HD
    own_head = row_head == lane_head
    is_key = lax.broadcasted_iota(jnp.int32, (heads * rows, key_rows), 1) % (2 * rows) < rows
    outs = []
    for i, query in enumerate((q_mine, q_x[...])):
        block = kv[:, :, i].reshape(key_rows, heads_half)
        spread = jnp.where(own_head, jnp.concatenate([query] * heads, axis=0), 0.0).astype(BF16)
        scores = dot_nt(spread, block) * (HD ** -0.5)
        scores = jnp.where(is_key, scores, -1e30)
        top = jnp.max(scores, axis=-1, keepdims=True)
        exp_scores = jnp.where(is_key, jnp.exp(scores - top), 0.0)
        total = jnp.sum(exp_scores, axis=-1, keepdims=True)
        moved = pltpu.roll(exp_scores, rows, axis=1).astype(BF16)
        mixed = dot_nn(moved, block) / total
        outs.append(jnp.concatenate(
            [mixed[h * rows:(h + 1) * rows, h * HD:(h + 1) * HD] for h in range(heads)], axis=1))

    def by_image(mine, theirs):
        return jnp.concatenate(
            [jnp.where(first, mine, theirs), jnp.where(first, theirs, mine)], axis=0)

    def own_rows(both):
        return jnp.where(first, both[:rows], both[rows:])

    def other_rows(both):
        return jnp.where(first, both[rows:], both[:rows])

    weights[0].wait()
    part_s[...] = dot_nn(by_image(outs[0], outs[1]).astype(BF16), wo[...])
    send(part_s, part_r, sib_sem.at[3], sibling)
    arrived(part_r, sib_sem.at[3])
    projected = part_s[...] + part_r[...]
    attended = (by_image(residual, res_x[...]) + projected).astype(BF16).astype(F32)
    mean_sq = jnp.mean(attended * attended, axis=-1, keepdims=True)
    normed32 = attended * lax.rsqrt(mean_sq + EPS) * gain_ref[...].reshape(1, width)
    normed = normed32.astype(BF16)
    tok[0, 0, 0] = normed[:, :half]
    tok[0, 0, 1] = normed[:, half:]

    own = tok.at[0, 0, core]
    for d in steps[1:]:
        send(own, tok.at[groups - d, 0, core], tok_sem.at[groups - d, 0], at(d, 0, core))
    for k in range(1, MEMBERS):
        send(own, tok.at[0, MEMBERS - k, core], tok_sem.at[0, MEMBERS - k], at(0, k, core))

    mid = own_rows(attended)
    att_ref[0] = mid.astype(BF16)
    for number in (1, 2, 3):
        weights[number].wait()
    hidden = jax.nn.silu(dot_nt(normed, sg[...])) * dot_nt(normed, su[...])
    shared = dot_nn(hidden.astype(BF16), sd[...])
    sh_s[...] = stack_halves(other_rows(shared))
    send(sh_s, sh_r, sib_sem.at[4], sibling)

    tok_cut = half - half // 5

    def tok_part(d, k):
        return tok.at[d, k, core, :, pl.ds(0, tok_cut)]

    def tok_rest(d, k):
        return tok.at[d, k, core, :, pl.ds(tok_cut, half - tok_cut)]

    def tok_on(d):
        arrived(tok.at[d, 0, core], tok_sem.at[d, 0])
        for k in range(1, MEMBERS):
            back = MEMBERS - k
            send(tok_part(d, 0), tok_part(d, back), tok_sem.at[d, back], at(0, k, core))
        send(tok.at[d, 0, core], tok.at[d, 0, core], toks_sem.at[d, 0], sibling)

    for d in steps[1:2]:
        tok_on(d)
    for k in range(1, MEMBERS):
        arrived(tok.at[0, k, core], tok_sem.at[0, k])
        for d in steps[1:]:
            back = groups - d
            send(tok_rest(0, k), tok_rest(back, k), tokr_sem.at[back, k], at(d, 0, core))
        send(tok.at[0, k, core], tok.at[0, k, core], toks_sem.at[0, k], sibling)
    for d in steps[2:]:
        tok_on(d)

    mine_normed = own_rows(normed.astype(F32))
    logits = lax.dot_general(router_ref[...], mine_normed, (((1,), (1,)), ((), ())),
                             precision=lax.Precision.HIGHEST, preferred_element_type=F32)
    probs = jax.nn.sigmoid(logits)
    experts = lax.broadcasted_iota(jnp.int32, (groups, rows), 0)
    ids = ids_ref[0]
    named = (ids[0:1] == experts) | (ids[1:2] == experts)
    pair_weight = jnp.where(named, probs, 0.0)
    diagonal = (lax.broadcasted_iota(jnp.int32, (rows, rows), 0)
                == lax.broadcasted_iota(jnp.int32, (rows, rows), 1))
    base = mid + own_rows(shared)

    for number in (4, 5, 6):
        weights[number].wait()

    def pass_on(s):
        d = steps[s]
        for k in range(1, MEMBERS):
            arrived(tok_part(d, k), tok_sem.at[d, k])
            arrived(tok_rest(d, k), tokr_sem.at[d, k])
            send(tok.at[d, k, core], tok.at[d, k, core], toks_sem.at[d, k], sibling)

    def expert(slots, wanted):
        for s in wanted:
            for k in range(MEMBERS):
                if s or k:
                    arrived(tok.at[steps[s], k, other], toks_sem.at[steps[s], k])
        low, high = slots
        count = (high - low) * MEMBERS * 2 * rows
        left = tok[low:high, :, 0].reshape(count, half)
        right = tok[low:high, :, 1].reshape(count, half)
        gate = dot_nt(left, rg[:, :half]) + dot_nt(right, rg[:, half:])
        up = dot_nt(left, ru[:, :half]) + dot_nt(right, ru[:, half:])
        inner = (jax.nn.silu(gate) * up).astype(BF16)
        theirs = dot_nn(inner, rd[:, pl.ds(pl.multiple_of(other * half, 128), half)])
        half_s[low:high] = theirs.astype(BF16).reshape(high - low, -1, half)
        for s in wanted:
            d = steps[s]
            send(half_s.at[d], half_r.at[d], half_sem.at[d], sibling)
        mine = dot_nn(inner, rd[:, pl.ds(pl.multiple_of(core * half, 128), half)])
        half_own[low:high] = mine.reshape(high - low, -1, half)

    def to_plane(s):
        d = steps[s]
        arrived(half_r.at[d], half_sem.at[d])
        half_own[d] += half_r[d].astype(F32)
        for k in range(1, MEMBERS):
            plane_s[d, k] = half_own[d, pl.ds(k * 2 * rows, 2 * rows)].astype(BF16)
            send(plane_s.at[d, k], plane_r.at[d, MEMBERS - k], plane_sem.at[d, MEMBERS - k],
                 at(0, k, core))

    def to_line(s):
        d = steps[s]
        total = half_own[d, pl.ds(0, 2 * rows)]
        for k in range(1, MEMBERS):
            arrived(plane_r.at[d, k], plane_sem.at[d, k])
            total += plane_r[d, k].astype(F32)
        line_s[d, 1] = stack_halves(other_rows(total))
        back = (groups - d) % groups
        if s == 0:
            line_r[0, core] = stack_halves(own_rows(total))
        else:
            line_s[d, 0] = stack_halves(own_rows(total))
            send(line_s.at[d, 0], line_r.at[back, core], line_sem.at[back, core], at(d, 0, core))
        send(line_s.at[d, 1], line_r.at[back, core], line_sem.at[back, core], at(d, 0, other))

    far_first = list(range(groups - 1, 0, -1))
    expert((0, 1), [0])
    for s in range(1, groups):
        pass_on(s)
    to_plane(0)
    expert((1, groups), far_first)
    for s in far_first:
        to_plane(s)
    to_line(0)
    for s in far_first:
        to_line(s)

    arrived(sh_r, sib_sem.at[4])
    result = base + unstack_halves(sh_r[...])
    for s, d in enumerate(steps):
        if s == 0:
            arrived(line_r.at[0, other], line_sem.at[0, other])
        else:
            arrived(line_r.at[d, 0], line_sem.at[d, 0])
            arrived(line_r.at[d, 1], line_sem.at[d, 1])
        named_row = jnp.where(experts == (group + d) % groups, pair_weight, 0.0)
        named_row = jnp.sum(named_row, axis=0, keepdims=True)
        scale = jnp.sum(jnp.where(diagonal, named_row, 0.0), axis=1, keepdims=True)
        value = jnp.concatenate(
            [unstack_halves(line_r[d, 0]), unstack_halves(line_r[d, 1])], axis=1)
        result += scale * value
    out_ref[0] = result.astype(BF16)

    for copy in sent:
        copy.wait_send()


def finish(attended, block_out, att_ref, out_ref):
    att_ref[...] = attended[...]
    out_ref[...] = block_out[...]


def per_device(
    queries, fresh_keys, fresh_values, stale_keys, stale_values, residual, out_proj, norm_gain,
    router, expert_ids, routed_gate, routed_up, routed_down, shared_gate, shared_up, shared_down,
):
    groups = router.shape[1]
    rows, width = residual.shape[1:]
    half = width // 2
    heads_half = queries.shape[2] // 2
    pack = 2 * rows
    weights = (out_proj, routed_gate[0], routed_up[0], routed_down[0],
               shared_gate, shared_up, shared_down)
    order = (0, 1, 2, 3, 4, 5, 6)
    vmem = pl.BlockSpec(memory_space=pltpu.VMEM)
    hbm = pl.BlockSpec(memory_space=pl.ANY)
    dma = pltpu.SemaphoreType.DMA
    inputs = (queries, fresh_keys, fresh_values, stale_keys, stale_values, residual,
              norm_gain, router.T, jnp.transpose(expert_ids, (0, 2, 1)))
    scratch = [pltpu.VMEM(x.shape, x.dtype) for x in inputs]
    scratch += [pltpu.VMEM(weights[n].shape, BF16) for n in order]
    scratch += [
        pltpu.VMEM((pack, heads_half), BF16),
        pltpu.VMEM((2, pack, heads_half), BF16),
        pltpu.VMEM((rows, heads_half), F32),
        pltpu.VMEM((rows, width), F32),
        pltpu.VMEM((rows, heads_half), F32),
        pltpu.VMEM((rows, width), F32),
        pltpu.VMEM((groups, MEMBERS, 2, pack, heads_half), BF16),
        pltpu.VMEM((pack, width), F32),
        pltpu.VMEM((pack, width), F32),
        pltpu.VMEM((groups, MEMBERS, 2, pack, half), BF16),
        pltpu.VMEM((pack, half), BF16),
        pltpu.VMEM((pack, half), BF16),
        pltpu.VMEM((groups, MEMBERS * pack, half), BF16),
        pltpu.VMEM((groups, MEMBERS * pack, half), BF16),
        pltpu.VMEM((groups, MEMBERS * pack, half), F32),
        pltpu.VMEM((groups, MEMBERS, pack, half), BF16),
        pltpu.VMEM((groups, MEMBERS, pack, half), BF16),
        pltpu.VMEM((groups, 2, pack, half // 2), BF16),
        pltpu.VMEM((groups, 2, pack, half // 2), BF16),
        dma((len(inputs),)),
        dma((7,)),
        dma((send_count(groups),)),
        dma((5,)),
        dma((groups, MEMBERS, 2)),
        dma((groups, MEMBERS)),
        dma((groups, MEMBERS)),
        dma((groups, MEMBERS)),
        dma((groups, MEMBERS)),
        dma((groups,)),
        dma((groups, MEMBERS)),
        dma((groups, 2)),
    ]
    attended, block_out = pl.pallas_call(
        functools.partial(kernel, groups),
        out_shape=(
            jax.ShapeDtypeStruct(residual.shape, BF16),
            jax.ShapeDtypeStruct(residual.shape, BF16),
        ),
        in_specs=[hbm] * 16,
        out_specs=(vmem, vmem),
        scratch_shapes=scratch,
        compiler_params=pltpu.CompilerParams(
            collective_id=0, has_side_effects=True, vmem_limit_bytes=56 * 1024 * 1024
        ),
        name="block",
    )(*inputs, *weights)
    return pl.pallas_call(
        finish,
        out_shape=tuple(jax.ShapeDtypeStruct(x.shape, x.dtype) for x in (attended, block_out)),
        in_specs=[vmem] * 2,
        out_specs=(vmem, vmem),
        name="finish",
    )(attended, block_out)


def solution(mesh):
    tokens = P(("groups", "image"), "patch", None)
    in_specs = (
        (tokens,) * 6
        + (P("image", None), P(), P(), tokens)
        + (P("patch", "image", None),) * 3
        + (P("image", None),) * 3
    )
    return jax.shard_map(
        per_device, mesh=mesh, in_specs=in_specs, out_specs=(tokens, tokens), check_vma=False
    )
```

```python
import functools

import jax
import jax.numpy as jnp
from jax import lax
from jax.experimental import pallas as pl
from jax.experimental.pallas import tpu as pltpu
from jax.sharding import PartitionSpec as P

HD = 128
EPS = 1e-06
MEMBERS = 4
MESH = pl.DeviceIdType.MESH
F32 = jnp.float32
BF16 = jnp.bfloat16


def dot_nt(rows, weight):
    return lax.dot_general(rows, weight, (((1,), (1,)), ((), ())), preferred_element_type=F32)


def dot_nn(rows, weight):
    return lax.dot_general(rows, weight, (((1,), (0,)), ((), ())), preferred_element_type=F32)


def stack_halves(rows):
    width = rows.shape[1] // 2
    return jnp.concatenate([rows[:, :width], rows[:, width:]], axis=0).astype(BF16)


def unstack_halves(packed):
    rows = packed.astype(F32)
    count = rows.shape[0] // 2
    return jnp.concatenate([rows[:count], rows[count:]], axis=1)


def send_count(groups):
    others = groups - 1
    members = MEMBERS - 1
    kv = 4 + 2 * others + 2 * groups * members + others * members
    tokens = 1 + others + groups * members + others * members + groups * MEMBERS - 1
    results = 1 + groups + groups * members + 2 * others + 1
    return kv + tokens + results


def kernel(
    groups,
    q_hbm, fk_hbm, fv_hbm, sk_hbm, sv_hbm, res_hbm, gain_hbm, router_hbm, ids_hbm,
    wo_hbm, rg_hbm, ru_hbm, rd_hbm, sg_hbm, su_hbm, sd_hbm,
    att_ref, out_ref,
    q_ref, fk_ref, fv_ref, sk_ref, sv_ref, res_ref, gain_ref, router_ref, ids_ref,
    wo, rg, ru, rd, sg, su, sd,
    stale_own, sib_kv, sib_q, sib_res, q_x, res_x, kv,
    part_s, part_r, tok, sh_s, sh_r,
    half_s, half_r, half_own, plane_s, plane_r, line_s, line_r,
    in_sem, w_sem, send_sem, sib_sem, kv_sem, rest_sem, tok_sem, tokr_sem, toks_sem, half_sem, plane_sem, line_sem,
):
    patch = lax.axis_index("patch")
    core = lax.axis_index("image")
    other = 1 - core
    first = core == 0
    group = patch // MEMBERS
    member = patch % MEMBERS
    rows = q_ref.shape[1]
    heads_half = q_ref.shape[2] // 2
    width = res_ref.shape[2]
    half = width // 2

    def at(step_group, step_member, to_core):
        target = ((group + step_group) % groups) * MEMBERS + (member + step_member) % MEMBERS
        return {"patch": target, "image": to_core}

    sibling = at(0, 0, other)

    near = jnp.minimum(group, groups - 1 - group)
    forward = 1 - 2 * ((2 * group) // groups)
    steps = [0]
    for s in range(groups - 1):
        both = forward * (1 - 2 * (s % 2)) * (s // 2 + 1)
        rest = forward * (s - near + 1)
        steps.append((jnp.where(s < 2 * near, both, rest) + groups) % groups)

    barrier = pltpu.get_barrier_semaphore()
    greeted = [sibling]
    for d in range(1, groups):
        greeted += [at(d, 0, core), at(d, 0, other)]
    for k in range(1, MEMBERS):
        greeted += [at(0, k, core), at(0, k, other)]
    for target in greeted:
        pl.semaphore_signal(barrier, inc=1, device_id=target, device_id_type=MESH)

    loads = []
    pairs = [(sk_hbm, sk_ref), (sv_hbm, sv_ref), (fk_hbm, fk_ref), (fv_hbm, fv_ref)]
    pairs += [(q_hbm, q_ref), (res_hbm, res_ref), (gain_hbm, gain_ref)]
    pairs += [(router_hbm, router_ref), (ids_hbm, ids_ref)]
    for number, (src, dst) in enumerate(pairs):
        copy = pltpu.make_async_copy(src, dst, in_sem.at[number])
        copy.start()
        loads.append(copy)

    weights = []
    pairs = [(wo_hbm, wo), (sg_hbm, sg), (su_hbm, su), (sd_hbm, sd)]
    pairs += [(rg_hbm, rg), (ru_hbm, ru), (rd_hbm, rd)]
    for number, (src, dst) in enumerate(pairs):
        copy = pltpu.make_async_copy(src, dst, w_sem.at[number])
        copy.start()
        weights.append(copy)

    sent = []

    def send(src, dst, recv, target):
        copy = pltpu.make_async_remote_copy(
            src_ref=src, dst_ref=dst, send_sem=send_sem.at[len(sent)], recv_sem=recv,
            device_id=target, device_id_type=MESH,
        )
        copy.start()
        sent.append(copy)

    def arrived(ref, recv):
        pltpu.make_async_remote_copy(
            src_ref=ref, dst_ref=ref, send_sem=send_sem.at[0], recv_sem=recv,
            device_id=sibling, device_id_type=MESH,
        ).wait_recv()

    def split(ref):
        whole = ref[0].astype(F32)
        left, right = whole[:, :heads_half], whole[:, heads_half:]
        return jnp.where(first, left, right), jnp.where(first, right, left)

    loads[0].wait()
    loads[1].wait()
    sk_mine, sk_theirs = split(sk_ref)
    sv_mine, sv_theirs = split(sv_ref)
    stale_own[...] = jnp.concatenate([sk_mine, sv_mine], axis=0).astype(BF16)
    sib_kv[0] = jnp.concatenate([sk_theirs, sv_theirs], axis=0).astype(BF16)
    for load in loads[2:]:
        load.wait()
    fk_mine, fk_theirs = split(fk_ref)
    fv_mine, fv_theirs = split(fv_ref)
    kv[0, 0, 0] = jnp.concatenate([fk_mine, fv_mine], axis=0).astype(BF16)
    sib_kv[1] = jnp.concatenate([fk_theirs, fv_theirs], axis=0).astype(BF16)
    q_mine, q_theirs = split(q_ref)
    sib_q[...] = q_theirs
    residual = res_ref[0].astype(F32)
    sib_res[...] = residual

    pl.semaphore_wait(barrier, len(greeted))

    cut = heads_half - 2 * (heads_half // 5)
    for d in steps[1:]:
        send(stale_own, kv.at[groups - d, 0, 0], kv_sem.at[groups - d, 0, 0], at(d, 0, core))
        send(sib_kv.at[0], kv.at[groups - d, 0, 1], kv_sem.at[groups - d, 0, 1], at(d, 0, other))
    for k in range(1, MEMBERS):
        back = MEMBERS - k
        send(stale_own, kv.at[0, back, 0], kv_sem.at[0, back, 0], at(0, k, core))
        send(sib_kv.at[0], kv.at[0, back, 1], kv_sem.at[0, back, 1], at(0, k, other))
    send(sib_kv.at[1], kv.at[0, 0, 1], kv_sem.at[0, 0, 1], sibling)
    send(sib_q, q_x, sib_sem.at[1], sibling)
    send(sib_res, res_x, sib_sem.at[2], sibling)

    def kv_part(d, k, i):
        return kv.at[d, k, i, :, pl.ds(0, cut)]

    def kv_rest(d, k):
        return kv.at[d, k, :, :, pl.ds(cut, heads_half - cut)]

    def kv_on(d):
        for i in range(2):
            arrived(kv.at[d, 0, i], kv_sem.at[d, 0, i])
            for k in range(1, MEMBERS):
                back = MEMBERS - k
                send(kv_part(d, 0, i), kv_part(d, back, i), kv_sem.at[d, back, i], at(0, k, core))

    for d in steps[1:2]:
        kv_on(d)
    for k in range(1, MEMBERS):
        for i in range(2):
            arrived(kv.at[0, k, i], kv_sem.at[0, k, i])
        for d in steps[1:]:
            send(kv_rest(0, k), kv_rest(groups - d, k), rest_sem.at[groups - d, k], at(d, 0, core))
    for d in steps[2:]:
        kv_on(d)
    arrived(q_x, sib_sem.at[1])
    arrived(res_x, sib_sem.at[2])
    arrived(kv.at[0, 0, 1], kv_sem.at[0, 0, 1])
    for d in steps[1:]:
        for k in range(1, MEMBERS):
            for i in range(2):
                arrived(kv_part(d, k, i), kv_sem.at[d, k, i])
            arrived(kv_rest(d, k), rest_sem.at[d, k])

    heads = heads_half // HD
    key_rows = groups * MEMBERS * 2 * rows
    row_head = lax.broadcasted_iota(jnp.int32, (heads * rows, heads_half), 0) // rows
    lane_head = lax.broadcasted_iota(jnp.int32, (heads * rows, heads_half), 1) // HD
    own_head = row_head == lane_head
    is_key = lax.broadcasted_iota(jnp.int32, (heads * rows, key_rows), 1) % (2 * rows) < rows
    outs = []
    for i, query in enumerate((q_mine, q_x[...])):
        block = kv[:, :, i].reshape(key_rows, heads_half)
        spread = jnp.where(own_head, jnp.concatenate([query] * heads, axis=0), 0.0).astype(BF16)
        scores = dot_nt(spread, block) * (HD ** -0.5)
        scores = jnp.where(is_key, scores, -1e30)
        top = jnp.max(scores, axis=-1, keepdims=True)
        exp_scores = jnp.where(is_key, jnp.exp(scores - top), 0.0)
        total = jnp.sum(exp_scores, axis=-1, keepdims=True)
        moved = pltpu.roll(exp_scores, rows, axis=1).astype(BF16)
        mixed = dot_nn(moved, block) / total
        outs.append(jnp.concatenate(
            [mixed[h * rows:(h + 1) * rows, h * HD:(h + 1) * HD] for h in range(heads)], axis=1))

    def by_image(mine, theirs):
        return jnp.concatenate(
            [jnp.where(first, mine, theirs), jnp.where(first, theirs, mine)], axis=0)

    def own_rows(both):
        return jnp.where(first, both[:rows], both[rows:])

    def other_rows(both):
        return jnp.where(first, both[rows:], both[:rows])

    weights[0].wait()
    part_s[...] = dot_nn(by_image(outs[0], outs[1]).astype(BF16), wo[...])
    send(part_s, part_r, sib_sem.at[3], sibling)
    arrived(part_r, sib_sem.at[3])
    projected = part_s[...] + part_r[...]
    attended = (by_image(residual, res_x[...]) + projected).astype(BF16).astype(F32)
    mean_sq = jnp.mean(attended * attended, axis=-1, keepdims=True)
    normed32 = attended * lax.rsqrt(mean_sq + EPS) * gain_ref[...].reshape(1, width)
    normed = normed32.astype(BF16)
    tok[0, 0, 0] = normed[:, :half]
    tok[0, 0, 1] = normed[:, half:]

    own = tok.at[0, 0, core]
    for d in steps[1:]:
        send(own, tok.at[groups - d, 0, core], tok_sem.at[groups - d, 0], at(d, 0, core))
    for k in range(1, MEMBERS):
        send(own, tok.at[0, MEMBERS - k, core], tok_sem.at[0, MEMBERS - k], at(0, k, core))

    mid = own_rows(attended)
    att_ref[0] = mid.astype(BF16)
    for number in (1, 2, 3):
        weights[number].wait()
    hidden = jax.nn.silu(dot_nt(normed, sg[...])) * dot_nt(normed, su[...])
    shared = dot_nn(hidden.astype(BF16), sd[...])
    sh_s[...] = stack_halves(other_rows(shared))
    send(sh_s, sh_r, sib_sem.at[4], sibling)

    tok_cut = half - 3 * (half // 10)

    def tok_part(d, k):
        return tok.at[d, k, core, :, pl.ds(0, tok_cut)]

    def tok_rest(d, k):
        return tok.at[d, k, core, :, pl.ds(tok_cut, half - tok_cut)]

    def tok_on(d):
        arrived(tok.at[d, 0, core], tok_sem.at[d, 0])
        for k in range(1, MEMBERS):
            back = MEMBERS - k
            send(tok_part(d, 0), tok_part(d, back), tok_sem.at[d, back], at(0, k, core))
        send(tok.at[d, 0, core], tok.at[d, 0, core], toks_sem.at[d, 0], sibling)

    for d in steps[1:2]:
        tok_on(d)
    for k in range(1, MEMBERS):
        arrived(tok.at[0, k, core], tok_sem.at[0, k])
        for d in steps[1:]:
            back = groups - d
            send(tok_rest(0, k), tok_rest(back, k), tokr_sem.at[back, k], at(d, 0, core))
        send(tok.at[0, k, core], tok.at[0, k, core], toks_sem.at[0, k], sibling)
    for d in steps[2:]:
        tok_on(d)

    mine_normed = own_rows(normed.astype(F32))
    logits = lax.dot_general(router_ref[...], mine_normed, (((1,), (1,)), ((), ())),
                             precision=lax.Precision.HIGHEST, preferred_element_type=F32)
    probs = jax.nn.sigmoid(logits)
    experts = lax.broadcasted_iota(jnp.int32, (groups, rows), 0)
    ids = ids_ref[0]
    named = (ids[0:1] == experts) | (ids[1:2] == experts)
    pair_weight = jnp.where(named, probs, 0.0)
    diagonal = (lax.broadcasted_iota(jnp.int32, (rows, rows), 0)
                == lax.broadcasted_iota(jnp.int32, (rows, rows), 1))
    base = mid + own_rows(shared)

    for number in (4, 5, 6):
        weights[number].wait()

    def pass_on(s):
        d = steps[s]
        for k in range(1, MEMBERS):
            arrived(tok_part(d, k), tok_sem.at[d, k])
            arrived(tok_rest(d, k), tokr_sem.at[d, k])
            send(tok.at[d, k, core], tok.at[d, k, core], toks_sem.at[d, k], sibling)

    def expert(slots, wanted):
        for s in wanted:
            for k in range(MEMBERS):
                if s or k:
                    arrived(tok.at[steps[s], k, other], toks_sem.at[steps[s], k])
        low, high = slots
        count = (high - low) * MEMBERS * 2 * rows
        left = tok[low:high, :, 0].reshape(count, half)
        right = tok[low:high, :, 1].reshape(count, half)
        gate = dot_nt(left, rg[:, :half]) + dot_nt(right, rg[:, half:])
        up = dot_nt(left, ru[:, :half]) + dot_nt(right, ru[:, half:])
        inner = (jax.nn.silu(gate) * up).astype(BF16)
        theirs = dot_nn(inner, rd[:, pl.ds(pl.multiple_of(other * half, 128), half)])
        half_s[low:high] = theirs.astype(BF16).reshape(high - low, -1, half)
        for s in wanted:
            d = steps[s]
            send(half_s.at[d], half_r.at[d], half_sem.at[d], sibling)
        mine = dot_nn(inner, rd[:, pl.ds(pl.multiple_of(core * half, 128), half)])
        half_own[low:high] = mine.reshape(high - low, -1, half)

    def to_plane(s):
        d = steps[s]
        arrived(half_r.at[d], half_sem.at[d])
        half_own[d] += half_r[d].astype(F32)
        for k in range(1, MEMBERS):
            plane_s[d, k] = half_own[d, pl.ds(k * 2 * rows, 2 * rows)].astype(BF16)
            send(plane_s.at[d, k], plane_r.at[d, MEMBERS - k], plane_sem.at[d, MEMBERS - k],
                 at(0, k, core))

    def to_line(s):
        d = steps[s]
        total = half_own[d, pl.ds(0, 2 * rows)]
        for k in range(1, MEMBERS):
            arrived(plane_r.at[d, k], plane_sem.at[d, k])
            total += plane_r[d, k].astype(F32)
        line_s[d, 1] = stack_halves(other_rows(total))
        back = (groups - d) % groups
        if s == 0:
            line_r[0, core] = stack_halves(own_rows(total))
        else:
            line_s[d, 0] = stack_halves(own_rows(total))
            send(line_s.at[d, 0], line_r.at[back, core], line_sem.at[back, core], at(d, 0, core))
        send(line_s.at[d, 1], line_r.at[back, core], line_sem.at[back, core], at(d, 0, other))

    far_first = list(range(groups - 1, 0, -1))
    expert((0, 1), [0])
    for s in range(1, groups):
        pass_on(s)
    to_plane(0)
    expert((1, groups), far_first)
    for s in far_first:
        to_plane(s)
    to_line(0)
    for s in far_first:
        to_line(s)

    arrived(sh_r, sib_sem.at[4])
    result = base + unstack_halves(sh_r[...])
    for s, d in enumerate(steps):
        if s == 0:
            arrived(line_r.at[0, other], line_sem.at[0, other])
        else:
            arrived(line_r.at[d, 0], line_sem.at[d, 0])
            arrived(line_r.at[d, 1], line_sem.at[d, 1])
        named_row = jnp.where(experts == (group + d) % groups, pair_weight, 0.0)
        named_row = jnp.sum(named_row, axis=0, keepdims=True)
        scale = jnp.sum(jnp.where(diagonal, named_row, 0.0), axis=1, keepdims=True)
        value = jnp.concatenate(
            [unstack_halves(line_r[d, 0]), unstack_halves(line_r[d, 1])], axis=1)
        result += scale * value
    out_ref[0] = result.astype(BF16)

    for copy in sent:
        copy.wait_send()


def finish(attended, block_out, att_ref, out_ref):
    att_ref[...] = attended[...]
    out_ref[...] = block_out[...]


def per_device(
    queries, fresh_keys, fresh_values, stale_keys, stale_values, residual, out_proj, norm_gain,
    router, expert_ids, routed_gate, routed_up, routed_down, shared_gate, shared_up, shared_down,
):
    groups = router.shape[1]
    rows, width = residual.shape[1:]
    half = width // 2
    heads_half = queries.shape[2] // 2
    pack = 2 * rows
    weights = (out_proj, routed_gate[0], routed_up[0], routed_down[0],
               shared_gate, shared_up, shared_down)
    order = (0, 1, 2, 3, 4, 5, 6)
    vmem = pl.BlockSpec(memory_space=pltpu.VMEM)
    hbm = pl.BlockSpec(memory_space=pl.ANY)
    dma = pltpu.SemaphoreType.DMA
    inputs = (queries, fresh_keys, fresh_values, stale_keys, stale_values, residual,
              norm_gain, router.T, jnp.transpose(expert_ids, (0, 2, 1)))
    scratch = [pltpu.VMEM(x.shape, x.dtype) for x in inputs]
    scratch += [pltpu.VMEM(weights[n].shape, BF16) for n in order]
    scratch += [
        pltpu.VMEM((pack, heads_half), BF16),
        pltpu.VMEM((2, pack, heads_half), BF16),
        pltpu.VMEM((rows, heads_half), F32),
        pltpu.VMEM((rows, width), F32),
        pltpu.VMEM((rows, heads_half), F32),
        pltpu.VMEM((rows, width), F32),
        pltpu.VMEM((groups, MEMBERS, 2, pack, heads_half), BF16),
        pltpu.VMEM((pack, width), F32),
        pltpu.VMEM((pack, width), F32),
        pltpu.VMEM((groups, MEMBERS, 2, pack, half), BF16),
        pltpu.VMEM((pack, half), BF16),
        pltpu.VMEM((pack, half), BF16),
        pltpu.VMEM((groups, MEMBERS * pack, half), BF16),
        pltpu.VMEM((groups, MEMBERS * pack, half), BF16),
        pltpu.VMEM((groups, MEMBERS * pack, half), F32),
        pltpu.VMEM((groups, MEMBERS, pack, half), BF16),
        pltpu.VMEM((groups, MEMBERS, pack, half), BF16),
        pltpu.VMEM((groups, 2, pack, half // 2), BF16),
        pltpu.VMEM((groups, 2, pack, half // 2), BF16),
        dma((len(inputs),)),
        dma((7,)),
        dma((send_count(groups),)),
        dma((5,)),
        dma((groups, MEMBERS, 2)),
        dma((groups, MEMBERS)),
        dma((groups, MEMBERS)),
        dma((groups, MEMBERS)),
        dma((groups, MEMBERS)),
        dma((groups,)),
        dma((groups, MEMBERS)),
        dma((groups, 2)),
    ]
    attended, block_out = pl.pallas_call(
        functools.partial(kernel, groups),
        out_shape=(
            jax.ShapeDtypeStruct(residual.shape, BF16),
            jax.ShapeDtypeStruct(residual.shape, BF16),
        ),
        in_specs=[hbm] * 16,
        out_specs=(vmem, vmem),
        scratch_shapes=scratch,
        compiler_params=pltpu.CompilerParams(
            collective_id=0, has_side_effects=True, vmem_limit_bytes=56 * 1024 * 1024
        ),
        name="block",
    )(*inputs, *weights)
    return pl.pallas_call(
        finish,
        out_shape=tuple(jax.ShapeDtypeStruct(x.shape, x.dtype) for x in (attended, block_out)),
        in_specs=[vmem] * 2,
        out_specs=(vmem, vmem),
        name="finish",
    )(attended, block_out)


def solution(mesh):
    tokens = P(("groups", "image"), "patch", None)
    in_specs = (
        (tokens,) * 6
        + (P("image", None), P(), P(), tokens)
        + (P("patch", "image", None),) * 3
        + (P("image", None),) * 3
    )
    return jax.shard_map(
        per_device, mesh=mesh, in_specs=in_specs, out_specs=(tokens, tokens), check_vma=False
    )
```
